32 devices in a mesh: group: 2 (over y), samp: 4 (over z), site: 2 (over x), sub: 2 (over core).
Axes of the slice: x: 2, y: 2, z: 4, core: 2. Of those that a mesh axis runs over, the one named last changes fastest.
Arguments:
- points: bfloat16 [1280, 16384], P(('group', 'samp'), ('site', 'sub')), parts along dimension 0, may hold values from -6 to 6
- scores: bfloat16 [1280, 16384], P(('group', 'samp'), ('site', 'sub')), parts along dimension 0, may hold values from -6 to 6
- target: bfloat16 [1280], P(('group', 'samp')), parts along dimension 0, may hold values from -6 to 13.5
Outputs:
- coeff: float32 [1280], P(('group', 'samp')), parts along dimension 0
- residual: float32 [1280], P(('group', 'samp')), parts along dimension 0
The draws below stay inside these ranges and needn't reach their ends.
There are 2 independent parts, one for each index of `group`. The reference program is written for one: setup_inputs(seed, part) draws one part's arguments, and reference() takes and returns one part's arrays. A program takes and returns all parts, laid end to end along the dimension named above; each array names one. Nothing has to cross between parts.
All inputs are finite; a program needn't handle non-finite values.
Results may differ from the reference program's by a relative error of at most 0.0003.
Values may be sent and summed in bfloat16 or wider, within the bound.
A program may use at most 64 MiB of HBM per device.

```python
import jax
import jax.numpy as jnp
from jax import lax

SITES = 16384
SAMPLES = 640


def draw_target(key, part):
    key = jax.random.fold_in(key, 7)
    position = jnp.arange(SAMPLES, dtype=jnp.float32) / float(SAMPLES - 1)
    raw = jnp.clip(jax.random.normal(key, (SAMPLES,), jnp.float32), -3.0, 3.0)
    offset = 1.0
    raw = raw.at[SAMPLES - 2].set(-3.0).at[SAMPLES - 1].set(3.0)
    return ((raw + offset) * jnp.power(3.0, position)).astype(jnp.bfloat16)


def block_levels(rng, extent, split, smallest, largest):
    level, own = 1.0, jax.random.fold_in(rng, 6)
    for dim, blocks in split:
        steps = jnp.exp(jax.random.uniform(jax.random.fold_in(own, dim), (blocks,), jnp.float32, smallest / len(split), largest / len(split)))
        level = level * jnp.repeat(steps, extent[dim] // blocks).reshape([-1 if axis == dim else 1 for axis in range(len(extent))])
    return level


def bell_draw(stream_key, extent, scale, limit, split=(), kind=jnp.bfloat16):
    result = scale * jax.random.normal(stream_key, extent, jnp.float32)
    if split:
        result = result * block_levels(stream_key, extent, split, -0.22, 0.18)
    return jnp.clip(result, -limit, limit).astype(kind)


def setup_inputs(seed: int = 0, part: int = 0) -> dict:
    streams_of = jax.random.split(jax.random.key(seed), 4)
    own_keys = jax.random.split(jax.random.fold_in(streams_of[3], part), 4)
    points = bell_draw(own_keys[0], (SAMPLES, SITES), 1.0, 6.0, ((0, 4), (1, 4)))
    scores = bell_draw(own_keys[1], (SAMPLES, SITES), 1.0, 6.0, ((0, 4), (1, 4)))
    target = draw_target(jax.random.fold_in(jax.random.fold_in(streams_of[3], part), 71), part)
    return dict(points=points, scores=scores, target=target)


RIDGE = 0.5


def reference(points, scores, target):
    width = float(SITES)
    pf = points.astype(jnp.float32)
    xx = jnp.sum(pf * pf, axis=1)
    gram = jnp.dot(points, points.T, preferred_element_type=jnp.float32)
    score_gram = jnp.dot(scores, scores.T, preferred_element_type=jnp.float32)
    sq_dist = xx[:, None] + xx[None, :] - 2.0 * gram
    kernel = jnp.exp(-sq_dist / (2.0 * width)) * (score_gram + 1.0) / width
    values = target.astype(jnp.float32)
    image = jnp.dot(kernel, values, precision=lax.Precision.HIGHEST) + RIDGE * values
    norm_sq = jnp.sum(values * values)
    curvature = jnp.sum(values * image)
    alpha = norm_sq / curvature
    return alpha * values, values - alpha * image
```

```python
import functools

import jax
import jax.numpy as jnp
from jax import lax
from jax.experimental import pallas as pl
from jax.experimental.pallas import tpu as pltpu
from jax.sharding import PartitionSpec as P

SITES = 16384


RIDGE = 0.5


def from_behind(value, axis, steps):
    count = lax.axis_size(axis)
    pairs = [(source, (source + steps) % count) for source in range(count)]
    return lax.ppermute(value, axis, pairs)


def partial_tiles(own_points, own_scores, vis_points, vis_scores):
    spec = (((1,), (1,)), ((), ()))
    gram = lax.dot_general(own_points, vis_points, spec, preferred_element_type=jnp.float32)
    score_gram = lax.dot_general(own_scores, vis_scores, spec, preferred_element_type=jnp.float32)
    return (gram, score_gram)


def stein_block(gram, score_gram, row_norms, col_norms, width):
    sq_dist = row_norms[:, None] + col_norms[None, :] - 2.0 * gram
    return jnp.exp(-sq_dist / (2.0 * width)) * (score_gram + 1.0) / width


def kernel_rows(own_points, own_scores, vis_points, vis_scores, row_norms, col_norms, width):
    parts = partial_tiles(own_points, own_scores, vis_points, vis_scores)
    gram, score_gram = lax.psum((parts[0], parts[1]), ("site", "sub"))
    return stein_block(gram, score_gram, row_norms, col_norms, width)


def ring_body(points, scores, target):
    count = points.shape[0]
    width = float(SITES)
    highest = lax.Precision.HIGHEST
    values = target.astype(jnp.float32)
    norm_sq = lax.psum(jnp.sum(values * values), "samp")
    self_sq = jnp.einsum("ik,ik->i", points, points, preferred_element_type=jnp.float32)
    own_norms = lax.psum(self_sq, ("site", "sub"))
    every_norms = lax.all_gather(own_norms, "samp", axis=0, tiled=True)
    cycle_size = lax.axis_size("samp")
    position = lax.axis_index("samp")

    def visitor_norms(step):
        owner = (position - step) % cycle_size
        return lax.dynamic_slice_in_dim(every_norms, owner * count, count, 0)

    block = kernel_rows(points, scores, points, scores, own_norms, own_norms, width)
    image = jnp.dot(block, values, precision=highest)
    owed = None
    half = cycle_size // 2

    def half_step(step, carry):
        vis_points, vis_scores, vis_target, carried, image_now = carry
        vis_points, vis_scores, vis_target = from_behind(
            (vis_points, vis_scores, vis_target), "samp", 1
        )
        tile = kernel_rows(
            points, scores, vis_points, vis_scores, own_norms, visitor_norms(step), width
        )
        image_now = image_now + jnp.dot(tile, vis_target.astype(jnp.float32), precision=highest)
        carried = carried + jnp.dot(values, tile, precision=highest)
        carried = from_behind(carried, "samp", 1)
        return (vis_points, vis_scores, vis_target, carried, image_now)

    start = (points, scores, target, jnp.zeros((count,), jnp.float32), image)
    vis_points, vis_scores, vis_target, carried, image = lax.fori_loop(1, half, half_step, start)
    owed = from_behind(carried, "samp", -half)
    vis_points, vis_scores, vis_target = from_behind(
        (vis_points, vis_scores, vis_target), "samp", 1
    )
    tile = kernel_rows(
        points, scores, vis_points, vis_scores, own_norms, visitor_norms(half), width
    )
    image = image + jnp.dot(tile, vis_target.astype(jnp.float32), precision=highest)
    image = image + owed
    image = image + RIDGE * values
    curvature = lax.psum(jnp.sum(values * image), "samp")
    alpha = norm_sq / curvature
    return (alpha * values, values - alpha * image)


MESH = pl.DeviceIdType.MESH
LANES = 128
F32 = jnp.float32


def spread(col, row_ids, col_ids):
    return jnp.sum(jnp.where(row_ids == col_ids, col, 0.0), axis=0, keepdims=True)


def stand(row, row_ids, col_ids):
    return jnp.sum(jnp.where(row_ids == col_ids, row, 0.0), axis=1, keepdims=True)


def ids(n):
    return (
        lax.broadcasted_iota(jnp.int32, (n, n), 0),
        lax.broadcasted_iota(jnp.int32, (n, n), 1),
    )


def fused_kernel(
    nz,
    points,
    scores,
    target,
    coeff,
    residual,
    gathered,
    own_points,
    tiles,
    core_in,
    samp_in,
    piece,
    site_in,
    vec_out,
    vec_in,
    img_out,
    img_in,
    norm_col,
    value_col,
    image_col,
    norm_row,
    value_row,
    local_sem,
    data_send,
    data_recv,
    vec_send,
    vec_recv,
    img_send,
    img_recv,
    core_sem,
    samp_send,
    samp_recv,
    site_sem,
):
    z = lax.axis_index("samp")
    x = lax.axis_index("site")
    c = lax.axis_index("sub")
    peers = 4 * nz
    me = (c * nz + z) * 2 + x
    count = target.shape[1]
    total = nz * count
    nb = total // LANES
    span = points.shape[1] // nz
    share = LANES // 2
    rows = share // nz
    half = rows // 2

    def where(p):
        return {"sub": p // (2 * nz), "samp": (p // 2) % nz, "site": p % 2}

    barrier = pltpu.get_barrier_semaphore()
    for k in range(1, peers):
        pl.semaphore_signal(
            barrier, inc=1, device_id=where((me + k) % peers), device_id_type=MESH
        )
    pl.semaphore_wait(barrier, peers - 1)

    def strip(kind, to):
        ref = points if kind == 0 else scores
        return ref.at[:, pl.ds(pl.multiple_of(span * to, span), span)]

    def slot(source_z, source_x):
        return gathered.at[
            source_x, pl.ds(pl.multiple_of(count * source_z, count), count), :
        ]

    def send_data(kind, to, number):
        return pltpu.make_async_remote_copy(
            src_ref=strip(kind, to),
            dst_ref=slot(z, x),
            send_sem=data_send.at[number],
            recv_sem=data_recv.at[z, x],
            device_id={"samp": to, "site": kind},
            device_id_type=MESH,
        )

    order = [(z + nz // 2) % nz] + [(z + k) % nz for k in range(1, nz) if k != nz // 2]
    if nz == 4:
        order = [(z + 2) % 4, 3 - z, z + 1 - 2 * (z % 2)]
    sends = []
    for to in order:
        for kind in (0, 1):
            sends.append(send_data(kind, to, len(sends)))
            sends[-1].start()

    def same_chip(kind):
        keep = pltpu.make_async_copy(strip(kind, z), slot(z, x), local_sem.at[1])
        give = send_data(1 - kind, z, 2 * nz - 2)
        return keep, give

    for kind in (0, 1):

        @pl.when(x == kind)
        def _():
            for copy in same_chip(kind):
                copy.start()

    fetch = pltpu.make_async_copy(points, own_points, local_sem.at[0])
    fetch.start()
    fetch.wait()
    wide = 512
    self_sq = jnp.zeros((count, 1), F32)
    for k in range(points.shape[1] // wide):
        part = own_points[:, wide * k : wide * (k + 1)].astype(F32)
        self_sq = self_sq + jnp.sum(part * part, axis=1, keepdims=True)
    row_ids, col_ids = ids(count)
    eye_row, eye_col = ids(LANES)
    vec_out[...] = jnp.zeros_like(vec_out)
    vec_out[0:1, 0:count] = spread(self_sq, row_ids, col_ids)
    vec_out[1:2, 0:count] = target[...]

    def send_vec(source, to, number):
        return pltpu.make_async_remote_copy(
            src_ref=vec_out,
            dst_ref=vec_in.at[source],
            send_sem=vec_send.at[number],
            recv_sem=vec_recv.at[source],
            device_id=where(to),
            device_id_type=MESH,
        )

    for k in range(1, peers):
        send_vec(me, (me + k) % peers, k - 1).start()
    vec_in[me] = vec_out[...]
    for k in range(1, peers):
        send_vec((me + k) % peers, (me + k) % peers, k - 1).wait_recv()
    for k in range(nz):
        norms = jnp.zeros((1, count), F32)
        for i in range(2):
            for j in range(2):
                norms = norms + vec_in[(i * nz + k) * 2 + j, 0:1, 0:count]
        values = vec_in[2 * k, 1:2, 0:count]
        block = pl.ds(k * count, count)
        norm_col[block, :] = jnp.broadcast_to(stand(norms, row_ids, col_ids), (count, LANES))
        value_col[block, :] = jnp.broadcast_to(stand(values, row_ids, col_ids), (count, LANES))
    norm_row[...] = jnp.zeros_like(norm_row)
    value_row[...] = jnp.zeros_like(value_row)
    for b in range(nb):
        block = pl.ds(b * LANES, LANES)
        norm_row[b : b + 1, :] = spread(norm_col[block, :], eye_row, eye_col)
        value_row[b : b + 1, :] = spread(value_col[block, :], eye_row, eye_col)

    def arrival(source_z, source_x):
        return pltpu.make_async_remote_copy(
            src_ref=slot(source_z, source_x),
            dst_ref=slot(source_z, source_x),
            send_sem=data_send.at[0],
            recv_sem=data_recv.at[source_z, source_x],
            device_id={"samp": source_z, "site": 1 - x},
            device_id_type=MESH,
        )

    pltpu.make_async_copy(slot(z, x), slot(z, x), local_sem.at[1]).wait()
    arrival(z, 1 - x).wait_recv()
    for k in range(1, nz):
        for j in (0, 1):
            arrival((z + k) % nz, j).wait_recv()

    pairs = [(i, j) for i in range(nb) for j in range(i, nb)]
    for i in range(nb):
        panel = jnp.zeros((LANES, total - LANES * i), F32)
        for j in (0, 1):
            panel = panel + lax.dot_general(
                gathered[j, LANES * i : LANES * (i + 1), :],
                gathered[j, LANES * i : total, :],
                (((1,), (1,)), ((), ())),
                preferred_element_type=F32,
            )
        for j in range(i, nb):
            tiles[pairs.index((i, j))] = panel[:, LANES * (j - i) : LANES * (j - i + 1)]

    mine = pl.ds(pl.multiple_of(share * c, share), share)
    theirs = pl.ds(pl.multiple_of(share * (1 - c), share), share)
    to_core = pltpu.make_async_remote_copy(
        src_ref=tiles.at[:, theirs, :],
        dst_ref=core_in,
        send_sem=core_sem.at[0],
        recv_sem=core_sem.at[1],
        device_id={"sub": 1 - c},
        device_id_type=MESH,
    )
    to_core.start()
    to_core.wait_recv()
    core_in[...] = core_in[...] + tiles[:, mine, :]

    def send_piece(source, to, number):
        return pltpu.make_async_remote_copy(
            src_ref=core_in.at[:, pl.ds(pl.multiple_of(rows * to, rows), rows), :],
            dst_ref=samp_in.at[source],
            send_sem=samp_send.at[number],
            recv_sem=samp_recv.at[source],
            device_id={"samp": to},
            device_id_type=MESH,
        )

    for number, to in enumerate(order):
        send_piece(z, to, number).start()
    samp_in[z] = core_in[:, pl.ds(pl.multiple_of(rows * z, rows), rows), :]
    for k in range(1, nz):
        send_piece((z + k) % nz, (z + k) % nz, 0).wait_recv()
    summed = samp_in[0]
    for k in range(1, nz):
        summed = summed + samp_in[k]
    piece[...] = summed

    to_site = pltpu.make_async_remote_copy(
        src_ref=piece.at[:, pl.ds(pl.multiple_of(half * (1 - x), half), half), :],
        dst_ref=site_in,
        send_sem=site_sem.at[0],
        recv_sem=site_sem.at[1],
        device_id={"site": 1 - x},
        device_id_type=MESH,
    )
    to_site.start()
    to_site.wait_recv()
    here = piece[:, pl.ds(pl.multiple_of(half * x, half), half), :]
    there = site_in[...]
    gram = jnp.where(x == 0, here, there)
    score_gram = jnp.where(x == 0, there, here)

    width = float(SITES)
    lane = lax.broadcasted_iota(jnp.int32, (half, LANES), 1)
    over = [jnp.zeros((1, LANES), F32) for _ in range(nb)]
    down = jnp.zeros((half, LANES), F32)
    for i in range(nb):
        at = pl.ds(pl.multiple_of(LANES * i + share * c + rows * z + half * x, half), half)
        row_norms, row_values = norm_col[at, :], value_col[at, :]
        for j in range(i, nb):
            n = pairs.index((i, j))
            sq_dist = row_norms + norm_row[j : j + 1, :] - 2.0 * gram[n]
            kernel = jnp.exp(-sq_dist / (2.0 * width)) * (score_gram[n] + 1.0) / width
            over[j] = over[j] + jnp.sum(kernel * row_values, axis=0, keepdims=True)
            if j > i:
                terms = jnp.sum(kernel * value_row[j : j + 1, :], axis=1, keepdims=True)
                down = down + jnp.where(lane == i, terms, 0.0)
    img_out[...] = jnp.zeros_like(img_out)
    for j in range(nb):
        img_out[j : j + 1, :] = over[j]
    img_out[8 : 8 + half, :] = down

    def send_img(source, to, number):
        return pltpu.make_async_remote_copy(
            src_ref=img_out,
            dst_ref=img_in.at[source],
            send_sem=img_send.at[number],
            recv_sem=img_recv.at[source],
            device_id=where(to),
            device_id_type=MESH,
        )

    for k in range(1, peers):
        send_img(me, (me + k) % peers, k - 1).start()
    img_in[me] = img_out[...]
    for k in range(1, peers):
        send_img((me + k) % peers, (me + k) % peers, k - 1).wait_recv()
    across = img_in[0, 0:8, :]
    for p in range(1, peers):
        across = across + img_in[p, 0:8, :]
    below = jnp.concatenate([img_in[p, 8 : 8 + half, :] for p in range(peers)], axis=0)
    curvature = jnp.zeros((1, 1), F32)
    norm_sq = jnp.zeros((1, 1), F32)
    for i in range(nb):
        values = value_row[i : i + 1, :]
        image = across[i : i + 1, :] + spread(below[:, i : i + 1], eye_row, eye_col)
        image = image + RIDGE * values
        curvature = curvature + jnp.sum(values * image, axis=1, keepdims=True)
        norm_sq = norm_sq + jnp.sum(values * values, axis=1, keepdims=True)
        image_col[LANES * i : LANES * (i + 1), :] = jnp.broadcast_to(
            stand(image, eye_row, eye_col), (LANES, LANES)
        )
    alpha = norm_sq / curvature
    own = image_col[pl.ds(pl.multiple_of(count * z, count), count), 0:1]
    own_image = spread(own, row_ids, col_ids)
    coeff[...] = alpha * target[...]
    residual[...] = target[...] - alpha * own_image

    for copy in sends:
        copy.wait_send()
    send_data(0, z, 2 * nz - 2).wait_send()
    for k in range(1, peers):
        send_vec(me, (me + k) % peers, k - 1).wait_send()
        send_img(me, (me + k) % peers, k - 1).wait_send()
    to_core.wait_send()
    to_site.wait_send()
    for number, to in enumerate(order):
        send_piece(z, to, number).wait_send()


def fused_body(nz, points, scores, target):
    count, sites = points.shape
    total = nz * count
    nb = total // LANES
    blocks = nb * (nb + 1) // 2
    rows = LANES // 2 // nz
    peers = 4 * nz
    dma = pltpu.SemaphoreType.DMA
    vmem = pl.BlockSpec(memory_space=pltpu.VMEM)
    wide = -(-count // LANES) * LANES
    coeff, residual = pl.pallas_call(
        functools.partial(fused_kernel, nz),
        out_shape=[jax.ShapeDtypeStruct((1, count), F32)] * 2,
        in_specs=[pl.BlockSpec(memory_space=pl.ANY)] * 2 + [vmem],
        out_specs=[vmem, vmem],
        scratch_shapes=[
            pltpu.VMEM((2, total, sites // nz), points.dtype),
            pltpu.VMEM((count, sites), points.dtype),
            pltpu.VMEM((blocks, LANES, LANES), F32),
            pltpu.VMEM((blocks, LANES // 2, LANES), F32),
            pltpu.VMEM((nz, blocks, rows, LANES), F32),
            pltpu.VMEM((blocks, rows, LANES), F32),
            pltpu.VMEM((blocks, rows // 2, LANES), F32),
            pltpu.VMEM((8, wide), F32),
            pltpu.VMEM((peers, 8, wide), F32),
            pltpu.VMEM((16, LANES), F32),
            pltpu.VMEM((peers, 16, LANES), F32),
            pltpu.VMEM((total, LANES), F32),
            pltpu.VMEM((total, LANES), F32),
            pltpu.VMEM((total, LANES), F32),
            pltpu.VMEM((8, LANES), F32),
            pltpu.VMEM((8, LANES), F32),
            dma((2,)),
            dma((2 * nz - 1,)),
            dma((nz, 2)),
            dma((peers - 1,)),
            dma((peers,)),
            dma((peers - 1,)),
            dma((peers,)),
            dma((2,)),
            dma((nz - 1,)),
            dma((nz,)),
            dma((2,)),
        ],
        compiler_params=pltpu.CompilerParams(
            collective_id=0, has_side_effects=True, vmem_limit_bytes=40 * 2**20
        ),
        cost_estimate=pl.CostEstimate(
            flops=2 * total * total * sites // 2,
            bytes_accessed=4 * count * sites,
            transcendentals=0,
        ),
    )(points, scores, target.astype(F32).reshape(1, count))
    return coeff.reshape(count), residual.reshape(count)


def solution(mesh):
    sizes = dict(mesh.shape)

    def body(points, scores, target):
        nz = sizes["samp"]
        total = nz * points.shape[0]
        fits = (
            sizes["site"] == 2
            and sizes["sub"] == 2
            and nz == 4
            and points.shape[0] % 16 == 0
            and total % LANES == 0
            and total <= 8 * LANES
            and points.shape[1] % (nz * LANES) == 0
            and points.shape[1] % 512 == 0
        )
        if fits:
            return fused_body(nz, points, scores, target)
        return ring_body(points, scores, target)

    return jax.shard_map(
        body,
        mesh=mesh,
        in_specs=(
            P(("group", "samp"), ("site", "sub")),
            P(("group", "samp"), ("site", "sub")),
            P(("group", "samp")),
        ),
        out_specs=(P(("group", "samp")), P(("group", "samp"))),
        check_vma=False,
    )
```

```python
import functools

import jax
import jax.numpy as jnp
from jax import lax
from jax.experimental import pallas as pl
from jax.experimental.pallas import tpu as pltpu
from jax.sharding import PartitionSpec as P

SITES = 16384


RIDGE = 0.5


def from_behind(value, axis, steps):
    count = lax.axis_size(axis)
    pairs = [(source, (source + steps) % count) for source in range(count)]
    return lax.ppermute(value, axis, pairs)


def partial_tiles(own_points, own_scores, vis_points, vis_scores):
    spec = (((1,), (1,)), ((), ()))
    gram = lax.dot_general(own_points, vis_points, spec, preferred_element_type=jnp.float32)
    score_gram = lax.dot_general(own_scores, vis_scores, spec, preferred_element_type=jnp.float32)
    return (gram, score_gram)


def stein_block(gram, score_gram, row_norms, col_norms, width):
    sq_dist = row_norms[:, None] + col_norms[None, :] - 2.0 * gram
    return jnp.exp(-sq_dist / (2.0 * width)) * (score_gram + 1.0) / width


def kernel_rows(own_points, own_scores, vis_points, vis_scores, row_norms, col_norms, width):
    parts = partial_tiles(own_points, own_scores, vis_points, vis_scores)
    gram, score_gram = lax.psum((parts[0], parts[1]), ("site", "sub"))
    return stein_block(gram, score_gram, row_norms, col_norms, width)


def ring_body(points, scores, target):
    count = points.shape[0]
    width = float(SITES)
    highest = lax.Precision.HIGHEST
    values = target.astype(jnp.float32)
    norm_sq = lax.psum(jnp.sum(values * values), "samp")
    self_sq = jnp.einsum("ik,ik->i", points, points, preferred_element_type=jnp.float32)
    own_norms = lax.psum(self_sq, ("site", "sub"))
    every_norms = lax.all_gather(own_norms, "samp", axis=0, tiled=True)
    cycle_size = lax.axis_size("samp")
    position = lax.axis_index("samp")

    def visitor_norms(step):
        owner = (position - step) % cycle_size
        return lax.dynamic_slice_in_dim(every_norms, owner * count, count, 0)

    block = kernel_rows(points, scores, points, scores, own_norms, own_norms, width)
    image = jnp.dot(block, values, precision=highest)
    owed = None
    half = cycle_size // 2

    def half_step(step, carry):
        vis_points, vis_scores, vis_target, carried, image_now = carry
        vis_points, vis_scores, vis_target = from_behind(
            (vis_points, vis_scores, vis_target), "samp", 1
        )
        tile = kernel_rows(
            points, scores, vis_points, vis_scores, own_norms, visitor_norms(step), width
        )
        image_now = image_now + jnp.dot(tile, vis_target.astype(jnp.float32), precision=highest)
        carried = carried + jnp.dot(values, tile, precision=highest)
        carried = from_behind(carried, "samp", 1)
        return (vis_points, vis_scores, vis_target, carried, image_now)

    start = (points, scores, target, jnp.zeros((count,), jnp.float32), image)
    vis_points, vis_scores, vis_target, carried, image = lax.fori_loop(1, half, half_step, start)
    owed = from_behind(carried, "samp", -half)
    vis_points, vis_scores, vis_target = from_behind(
        (vis_points, vis_scores, vis_target), "samp", 1
    )
    tile = kernel_rows(
        points, scores, vis_points, vis_scores, own_norms, visitor_norms(half), width
    )
    image = image + jnp.dot(tile, vis_target.astype(jnp.float32), precision=highest)
    image = image + owed
    image = image + RIDGE * values
    curvature = lax.psum(jnp.sum(values * image), "samp")
    alpha = norm_sq / curvature
    return (alpha * values, values - alpha * image)


MESH = pl.DeviceIdType.MESH
LANES = 128
PARTS = 4
F32 = jnp.float32


def spread(col, row_ids, col_ids):
    return jnp.sum(jnp.where(row_ids == col_ids, col, 0.0), axis=0, keepdims=True)


def stand(row, row_ids, col_ids):
    return jnp.sum(jnp.where(row_ids == col_ids, row, 0.0), axis=1, keepdims=True)


def ids(n):
    return (
        lax.broadcasted_iota(jnp.int32, (n, n), 0),
        lax.broadcasted_iota(jnp.int32, (n, n), 1),
    )


def fused_kernel(
    nz,
    points,
    scores,
    target,
    result,
    gathered,
    own_points,
    tiles,
    core_in,
    pieces,
    vec_out,
    vec_in,
    img_out,
    img_in,
    norm_col,
    value_col,
    image_col,
    norm_row,
    value_row,
    local_sem,
    data_send,
    data_recv,
    vec_send,
    vec_recv,
    img_send,
    img_recv,
    core_sem,
    piece_send,
    piece_recv,
):
    z = lax.axis_index("samp")
    x = lax.axis_index("site")
    c = lax.axis_index("sub")
    peers = 4 * nz
    me = (c * nz + z) * 2 + x
    count = target.shape[0]
    total = nz * count
    nb = total // LANES
    span = points.shape[1] // nz
    parts = gathered.shape[0]
    sub = span // parts
    share = LANES // 2
    rows = share // nz
    half = rows // 2

    def where(p):
        return {"sub": p // (2 * nz), "samp": (p // 2) % nz, "site": p % 2}

    barrier = pltpu.get_barrier_semaphore()
    for k in range(1, peers):
        pl.semaphore_signal(
            barrier, inc=1, device_id=where((me + k) % peers), device_id_type=MESH
        )
    pl.semaphore_wait(barrier, peers - 1)

    def strip(kind, to, part):
        ref = points if kind == 0 else scores
        at = pl.multiple_of(span * to + sub * part, sub)
        return ref.at[:, pl.ds(at, sub)]

    def slot(source_z, source_x, part):
        return gathered.at[
            part, source_x, pl.ds(pl.multiple_of(count * source_z, count), count), :
        ]

    def send_data(kind, to, part, number):
        return pltpu.make_async_remote_copy(
            src_ref=strip(kind, to, part),
            dst_ref=slot(z, x, part),
            send_sem=data_send.at[part, number],
            recv_sem=data_recv.at[part, z, x],
            device_id={"samp": to, "site": kind},
            device_id_type=MESH,
        )

    order = [(z + nz // 2) % nz] + [(z + k) % nz for k in range(1, nz) if k != nz // 2]
    if nz == 4:
        order = [(z + 2) % 4, 3 - z, z + 1 - 2 * (z % 2)]
    sends = []

    def same_chip(kind, part):
        keep = pltpu.make_async_copy(
            strip(kind, z, part), slot(z, x, part), local_sem.at[1 + part]
        )
        give = send_data(1 - kind, z, part, 2 * nz - 2)
        return keep, give

    for part in range(parts):
        for n, to in enumerate(order):
            for kind in (0, 1):
                sends.append(send_data(kind, to, part, 2 * n + kind))
                sends[-1].start()
        for kind in (0, 1):

            @pl.when(x == kind)
            def _():
                for copy in same_chip(kind, part):
                    copy.start()

    fetch = pltpu.make_async_copy(points, own_points, local_sem.at[0])
    fetch.start()
    fetch.wait()
    wide = 512
    self_sq = jnp.zeros((count, 1), F32)
    for k in range(points.shape[1] // wide):
        part = own_points[:, wide * k : wide * (k + 1)].astype(F32)
        self_sq = self_sq + jnp.sum(part * part, axis=1, keepdims=True)
    row_ids, col_ids = ids(count)
    eye_row, eye_col = ids(LANES)
    vec_out[...] = jnp.zeros_like(vec_out)
    vec_out[0:1, 0:count] = spread(self_sq, row_ids, col_ids)
    vec_out[1:2, 0:count] = target[...].astype(F32).reshape(1, count)

    def send_vec(source, to, number):
        return pltpu.make_async_remote_copy(
            src_ref=vec_out,
            dst_ref=vec_in.at[source],
            send_sem=vec_send.at[number],
            recv_sem=vec_recv.at[source],
            device_id=where(to),
            device_id_type=MESH,
        )

    for k in range(1, peers):
        send_vec(me, (me + k) % peers, k - 1).start()
    vec_in[me] = vec_out[...]
    def arrival(source_z, source_x, part):
        return pltpu.make_async_remote_copy(
            src_ref=slot(source_z, source_x, part),
            dst_ref=slot(source_z, source_x, part),
            send_sem=data_send.at[part, 0],
            recv_sem=data_recv.at[part, source_z, source_x],
            device_id={"samp": source_z, "site": 1 - x},
            device_id_type=MESH,
        )

    pairs = [(i, j) for i in range(nb) for j in range(i, nb)]
    for part in range(parts):
        pltpu.make_async_copy(
            slot(z, x, part), slot(z, x, part), local_sem.at[1 + part]
        ).wait()
        arrival(z, 1 - x, part).wait_recv()
        for k in range(1, nz):
            for j in (0, 1):
                arrival((z + k) % nz, j, part).wait_recv()
        for i in range(nb):
            panel = jnp.zeros((LANES, total - LANES * i), F32)
            for j in (0, 1):
                panel = panel + lax.dot_general(
                    gathered[part, j, LANES * i : LANES * (i + 1), :],
                    gathered[part, j, LANES * i : total, :],
                    (((1,), (1,)), ((), ())),
                    preferred_element_type=F32,
                )
            for j in range(i, nb):
                block = panel[:, LANES * (j - i) : LANES * (j - i + 1)]
                n = pairs.index((i, j))
                tiles[n] = block if part == 0 else tiles[n] + block

    mine = pl.ds(pl.multiple_of(share * c, share), share)
    theirs = pl.ds(pl.multiple_of(share * (1 - c), share), share)
    to_core = pltpu.make_async_remote_copy(
        src_ref=tiles.at[:, theirs, :],
        dst_ref=core_in,
        send_sem=core_sem.at[0],
        recv_sem=core_sem.at[1],
        device_id={"sub": 1 - c},
        device_id_type=MESH,
    )
    to_core.start()
    to_core.wait_recv()
    core_in[...] = core_in[...] + tiles[:, mine, :]

    def piece_rows(to_z, to_x):
        return pl.ds(pl.multiple_of(rows * to_z + half * to_x, half), half)

    def send_piece(to_z, to_x, number):
        return pltpu.make_async_remote_copy(
            src_ref=core_in.at[:, piece_rows(to_z, to_x), :],
            dst_ref=pieces.at[x, z],
            send_sem=piece_send.at[number],
            recv_sem=piece_recv.at[x, z],
            device_id={"samp": to_z, "site": to_x},
            device_id_type=MESH,
        )

    def piece_arrival(source_z, source_x):
        return pltpu.make_async_remote_copy(
            src_ref=pieces.at[source_x, source_z],
            dst_ref=pieces.at[source_x, source_z],
            send_sem=piece_send.at[0],
            recv_sem=piece_recv.at[source_x, source_z],
            device_id={"samp": source_z, "site": 1 - x},
            device_id_type=MESH,
        )

    piece_sends = []
    for to in order:
        for kind in (1 - x, x):
            piece_sends.append(send_piece(to, kind, len(piece_sends)))
            piece_sends[-1].start()
    piece_sends.append(send_piece(z, 1 - x, len(piece_sends)))
    piece_sends[-1].start()
    pieces[x, z] = core_in[:, piece_rows(z, x), :]
    for k in range(1, peers):
        send_vec((me + k) % peers, (me + k) % peers, k - 1).wait_recv()
    for k in range(nz):
        norms = jnp.zeros((1, count), F32)
        for i in range(2):
            for j in range(2):
                norms = norms + vec_in[(i * nz + k) * 2 + j, 0:1, 0:count]
        values = vec_in[2 * k, 1:2, 0:count]
        block = pl.ds(k * count, count)
        norm_col[block, :] = jnp.broadcast_to(stand(norms, row_ids, col_ids), (count, LANES))
        value_col[block, :] = jnp.broadcast_to(stand(values, row_ids, col_ids), (count, LANES))
    norm_row[...] = jnp.zeros_like(norm_row)
    value_row[...] = jnp.zeros_like(value_row)
    for b in range(nb):
        block = pl.ds(b * LANES, LANES)
        norm_row[b : b + 1, :] = spread(norm_col[block, :], eye_row, eye_col)
        value_row[b : b + 1, :] = spread(value_col[block, :], eye_row, eye_col)
    piece_arrival(z, 1 - x).wait_recv()
    for k in range(1, nz):
        for j in (0, 1):
            piece_arrival((z + k) % nz, j).wait_recv()
    gram, score_gram = pieces[0, 0], pieces[1, 0]
    for k in range(1, nz):
        gram = gram + pieces[0, k]
        score_gram = score_gram + pieces[1, k]

    width = float(SITES)
    lane = lax.broadcasted_iota(jnp.int32, (half, LANES), 1)
    over = [jnp.zeros((1, LANES), F32) for _ in range(nb)]
    down = jnp.zeros((half, LANES), F32)
    for i in range(nb):
        at = pl.ds(pl.multiple_of(LANES * i + share * c + rows * z + half * x, half), half)
        row_norms, row_values = norm_col[at, :], value_col[at, :]
        for j in range(i, nb):
            n = pairs.index((i, j))
            sq_dist = row_norms + norm_row[j : j + 1, :] - 2.0 * gram[n]
            kernel = jnp.exp(-sq_dist / (2.0 * width)) * (score_gram[n] + 1.0) / width
            over[j] = over[j] + jnp.sum(kernel * row_values, axis=0, keepdims=True)
            if j > i:
                terms = jnp.sum(kernel * value_row[j : j + 1, :], axis=1, keepdims=True)
                down = down + jnp.where(lane == i, terms, 0.0)
    img_out[...] = jnp.zeros_like(img_out)
    for j in range(nb):
        img_out[j : j + 1, :] = over[j]
    img_out[8 : 8 + half, :] = down

    def send_img(source, to, number):
        return pltpu.make_async_remote_copy(
            src_ref=img_out,
            dst_ref=img_in.at[source],
            send_sem=img_send.at[number],
            recv_sem=img_recv.at[source],
            device_id=where(to),
            device_id_type=MESH,
        )

    for k in range(1, peers):
        send_img(me, (me + k) % peers, k - 1).start()
    img_in[me] = img_out[...]
    for k in range(1, peers):
        send_img((me + k) % peers, (me + k) % peers, k - 1).wait_recv()
    across = img_in[0, 0:8, :]
    for p in range(1, peers):
        across = across + img_in[p, 0:8, :]
    below = jnp.concatenate([img_in[p, 8 : 8 + half, :] for p in range(peers)], axis=0)
    curvature = jnp.zeros((1, 1), F32)
    norm_sq = jnp.zeros((1, 1), F32)
    for i in range(nb):
        values = value_row[i : i + 1, :]
        image = across[i : i + 1, :] + spread(below[:, i : i + 1], eye_row, eye_col)
        image = image + RIDGE * values
        curvature = curvature + jnp.sum(values * image, axis=1, keepdims=True)
        norm_sq = norm_sq + jnp.sum(values * values, axis=1, keepdims=True)
        image_col[LANES * i : LANES * (i + 1), :] = jnp.broadcast_to(
            stand(image, eye_row, eye_col), (LANES, LANES)
        )
    alpha = norm_sq / curvature
    own = image_col[pl.ds(pl.multiple_of(count * z, count), count), 0:1]
    own_image = spread(own, row_ids, col_ids)
    result[0:1, :] = own_image
    result[1:2, :] = jnp.broadcast_to(alpha, (1, count))

    for copy in sends:
        copy.wait_send()
    for part in range(parts):
        send_data(0, z, part, 2 * nz - 2).wait_send()
    for k in range(1, peers):
        send_vec(me, (me + k) % peers, k - 1).wait_send()
        send_img(me, (me + k) % peers, k - 1).wait_send()
    to_core.wait_send()
    for copy in piece_sends:
        copy.wait_send()


def fused_body(nz, points, scores, target):
    count, sites = points.shape
    total = nz * count
    nb = total // LANES
    blocks = nb * (nb + 1) // 2
    parts = PARTS
    rows = LANES // 2 // nz
    peers = 4 * nz
    dma = pltpu.SemaphoreType.DMA
    vmem = pl.BlockSpec(memory_space=pltpu.VMEM)
    wide = -(-count // LANES) * LANES
    result = pl.pallas_call(
        functools.partial(fused_kernel, nz),
        out_shape=jax.ShapeDtypeStruct((2, count), F32),
        in_specs=[pl.BlockSpec(memory_space=pl.ANY)] * 2 + [vmem],
        out_specs=vmem,
        scratch_shapes=[
            pltpu.VMEM((parts, 2, total, sites // nz // parts), points.dtype),
            pltpu.VMEM((count, sites), points.dtype),
            pltpu.VMEM((blocks, LANES, LANES), F32),
            pltpu.VMEM((blocks, LANES // 2, LANES), F32),
            pltpu.VMEM((2, nz, blocks, rows // 2, LANES), F32),
            pltpu.VMEM((8, wide), F32),
            pltpu.VMEM((peers, 8, wide), F32),
            pltpu.VMEM((16, LANES), F32),
            pltpu.VMEM((peers, 16, LANES), F32),
            pltpu.VMEM((total, LANES), F32),
            pltpu.VMEM((total, LANES), F32),
            pltpu.VMEM((total, LANES), F32),
            pltpu.VMEM((8, LANES), F32),
            pltpu.VMEM((8, LANES), F32),
            dma((1 + parts,)),
            dma((parts, 2 * nz - 1)),
            dma((parts, nz, 2)),
            dma((peers - 1,)),
            dma((peers,)),
            dma((peers - 1,)),
            dma((peers,)),
            dma((2,)),
            dma((2 * nz - 1,)),
            dma((2, nz)),
        ],
        compiler_params=pltpu.CompilerParams(
            collective_id=0, has_side_effects=True, vmem_limit_bytes=56 * 2**20
        ),
        cost_estimate=pl.CostEstimate(
            flops=2 * total * total * sites // 2,
            bytes_accessed=4 * count * sites,
            transcendentals=0,
        ),
    )(points, scores, target)
    values = target.astype(F32)
    image, alpha = result[0], result[1]
    return alpha * values, values - alpha * image


def solution(mesh):
    sizes = dict(mesh.shape)

    def body(points, scores, target):
        nz = sizes["samp"]
        total = nz * points.shape[0]
        fits = (
            sizes["site"] == 2
            and sizes["sub"] == 2
            and nz == 4
            and points.shape[0] % 16 == 0
            and total % LANES == 0
            and total <= 8 * LANES
            and points.shape[1] % (nz * PARTS * LANES) == 0
            and points.shape[1] % 512 == 0
        )
        if fits:
            return fused_body(nz, points, scores, target)
        return ring_body(points, scores, target)

    return jax.shard_map(
        body,
        mesh=mesh,
        in_specs=(
            P(("group", "samp"), ("site", "sub")),
            P(("group", "samp"), ("site", "sub")),
            P(("group", "samp")),
        ),
        out_specs=(P(("group", "samp")), P(("group", "samp"))),
        check_vma=False,
    )
```
